512 devices in a mesh: dp: 64 (over z, y_lo, core), tensor: 8 (over x, y_hi).
Axes of the slice: x: 4, y: 8 (y_hi: 2, y_lo: 4; y = y_hi * 4 + y_lo), z: 8, core: 2. Of those that a mesh axis runs over, the one named last changes fastest.
Arguments:
- token_features: bfloat16 [12288, 5120], P(('dp', 'tensor')), may hold values from -6 to 6
- key_cotangent: bfloat16 [12288, 1024], P('dp', 'tensor'), may hold values from -6 to 6
- weight_master: float32 [5120, 1024], P('dp', 'tensor'), may hold values from -20 to 20
- weight_first: float32 [5120, 1024], P('dp', 'tensor'), may hold values from -24 to 24
- weight_second: float32 [5120, 1024], P('dp', 'tensor'), may hold values from 1 to 100
- gain_master_copy: float32 [128, 8], P('dp', 'tensor'), may hold values from 0.25 to 1.75
- gain_first_moment: float32 [128, 8], P('dp', 'tensor'), may hold values from -24 to 24
- gain_second_moment: float32 [128, 8], P('dp', 'tensor'), may hold values from 1 to 100
- weight_grad_prev: bfloat16 [64, 5120, 1024], P('dp', None, 'tensor'), may hold values from -16 to 16
- prior_gain_gradient: float32 [64, 128, 8], P('dp', None, 'tensor'), may hold values from -16 to 16
Outputs:
- input_grad: bfloat16 [12288, 5120], P(('dp', 'tensor'))
- weight_grad: bfloat16 [64, 5120, 1024], P('dp', None, 'tensor')
- gain_grad: float32 [64, 128, 8], P('dp', None, 'tensor')
- new_weight: float32 [5120, 1024], P('dp', 'tensor')
- new_weight_first: float32 [5120, 1024], P('dp', 'tensor')
- new_weight_second: float32 [5120, 1024], P('dp', 'tensor')
- new_gain: float32 [128, 8], P('dp', 'tensor')
- new_gain_first: float32 [128, 8], P('dp', 'tensor')
- new_gain_second: float32 [128, 8], P('dp', 'tensor')
The draws below stay inside these ranges and needn't reach their ends.
All inputs are finite; a program needn't handle non-finite values.
Results may differ from the reference program's by a relative error of at most 0.012.
Values may be sent and summed in bfloat16 or wider, within the bound.
No kernel may reach another device: no remote copies, remote signals or barrier semaphores. Data moves between devices by JAX's collectives and lax.ppermute only.
A program may use at most 64 MiB of HBM per device.

```python
import math
import jax
import jax.numpy as jnp
from jax import lax

D = 5120
HEAD_WIDTH = 128
KEY_HEADS = 8
KEY_FEATURES = 1024
TOK_DEV = 192
TOKENS = 12288
N_DP = 64
N_TENSOR = 8


def draw_weight_master(key, part):
    key = jax.random.fold_in(key, 11)
    key_base, key_rows, key_cols = jax.random.split(key, 3)
    base = jnp.clip(jax.random.normal(key_base, (D, KEY_FEATURES), jnp.float32), -4.0, 4.0)
    row_scale = jnp.exp(jax.random.uniform(key_rows, (D, 1), jnp.float32) * math.log(10.0))
    col_scale = jnp.exp(jax.random.uniform(key_cols, (1, KEY_FEATURES), jnp.float32) * math.log(10.0))
    norm_level = (jnp.arange(KEY_FEATURES) // HEAD_WIDTH).astype(jnp.float32) / (KEY_HEADS - 1)
    rising = jnp.exp(norm_level * math.log(3.0))[None, :]
    return base * row_scale * col_scale * rising / math.sqrt(D)


def spiked(result, own_key, source, target, shards_of, factor):
    owner, partner = [(jnp.arange(result.shape[axis_at]) // (result.shape[axis_at] // shards_of)).reshape([-1 if axis == axis_at else 1 for axis in range(result.ndim)]) for axis_at in (source, target)]
    chosen = jax.random.permutation(own_key, shards_of)[partner]
    strong = (owner == chosen) | (owner == (partner + shards_of // 2) % shards_of)
    return jnp.where(strong, factor * result, result)


def level_of(rng, dims, shards, least, largest):
    factor_of, own = 1.0, jax.random.fold_in(rng, 6)
    for dim, blocks in shards:
        steps = jnp.exp(jax.random.uniform(jax.random.fold_in(own, dim), (blocks,), jnp.float32, least / len(shards), largest / len(shards)))
        factor_of = factor_of * jnp.repeat(steps, dims[dim] // blocks).reshape([-1 if axis == dim else 1 for axis in range(len(dims))])
    return factor_of


def centred(key, shape, spread, bound, cuts=(), kind=jnp.bfloat16):
    gain = level_of(key, shape, cuts, -0.22, 0.18) if cuts else 1.0
    values = jax.random.normal(key, shape, jnp.float32) * spread * gain
    return jnp.minimum(jnp.maximum(values, -bound), bound).astype(kind)


def noise_with(stream_key, shape, scale, reach, pieces, heavy, kind=jnp.bfloat16):
    entries = scale * jax.random.normal(stream_key, shape, jnp.float32)
    if pieces:
        entries = entries * level_of(stream_key, shape, pieces, -0.22, 0.18)
    return jnp.clip(spiked(entries, jax.random.fold_in(stream_key, 3), *heavy), -reach, reach).astype(kind)


def setup_inputs(seed: int = 0) -> dict:
    seeds = jax.random.split(jax.random.key(seed), 11)
    token_features = centred(seeds[0], (TOKENS, D), 1.0, 6.0, ((0, 512),))
    key_cotangent = centred(seeds[1], (TOKENS, KEY_FEATURES), 1.0, 6.0, ((0, 64), (1, 8)))
    weight_master = draw_weight_master(jax.random.fold_in(seeds[10], 71), 0)
    weight_first = centred(seeds[3], (D, KEY_FEATURES), 4.0, 24.0, ((0, 64), (1, 8)), jnp.float32)
    weight_second = jnp.clip(jnp.exp(math.log(100.0) - 4.6051702 * jax.random.uniform(seeds[4], (D, KEY_FEATURES), jnp.float32) ** level_of(seeds[4], (D, KEY_FEATURES), ((0, 64), (1, 8)), -0.2, 0.2)), 1.0, 100.0)
    gain_master_copy = jnp.clip(1.0 + 0.15 * jax.random.normal(seeds[5], (HEAD_WIDTH, KEY_HEADS), jnp.float32), 0.25, 1.75)
    gain_first_moment = centred(seeds[6], (HEAD_WIDTH, KEY_HEADS), 4.0, 24.0, ((0, 64), (1, 8)), jnp.float32)
    gain_second_moment = jnp.clip(jnp.exp(math.log(100.0) - 4.6051702 * jax.random.uniform(seeds[7], (HEAD_WIDTH, KEY_HEADS), jnp.float32) ** level_of(seeds[7], (HEAD_WIDTH, KEY_HEADS), ((0, 64), (1, 8)), -0.2, 0.2)), 1.0, 100.0)
    weight_grad_prev = noise_with(seeds[8], (N_DP, D, KEY_FEATURES), 1.0, 16.0, ((0, 64), (2, 8)), (0, 1, 64, 4.0))
    prior_gain_gradient = noise_with(seeds[9], (N_DP, HEAD_WIDTH, KEY_HEADS), 1.0, 16.0, ((0, 64), (2, 8)), (0, 1, 64, 4.0), jnp.float32)
    return {"token_features": token_features, "key_cotangent": key_cotangent, "weight_master": weight_master, "weight_first": weight_first, "weight_second": weight_second, "gain_master_copy": gain_master_copy, "gain_first_moment": gain_first_moment, "gain_second_moment": gain_second_moment, "weight_grad_prev": weight_grad_prev, "prior_gain_gradient": prior_gain_gradient}


beta_one = 0.9
beta_two = 0.95
corr_one = 1.0 - 0.9 ** 8
corr_two = 1.0 - 0.95 ** 8
learn_rate = 0.02
weight_decay = 0.1
adam_eps = 1e-08
norm_eps = 1e-06

def adamw(param, first, second, grad, decay):
    first_new = beta_one * first + (1.0 - beta_one) * grad
    second_new = beta_two * second + (1.0 - beta_two) * grad * grad
    update = first_new / corr_one / (jnp.sqrt(second_new / corr_two) + adam_eps)
    return (param - learn_rate * (update + decay * param), first_new, second_new)

def reference(token_features, key_cotangent, weight_master, weight_first, weight_second, gain_master_copy, gain_first_moment, gain_second_moment, weight_grad_prev, prior_gain_gradient):
    weights = weight_master.astype(jnp.bfloat16)
    gain_low = lax.optimization_barrier(gain_master_copy.astype(jnp.bfloat16))
    gain_vec = gain_low.astype(jnp.float32).T.reshape(KEY_FEATURES)
    width = KEY_FEATURES // N_TENSOR
    blocked_w = weights.reshape(D, N_TENSOR, width).astype(jnp.float32)

    def one_group(pair):
        rows, output_cotangent = pair
        keys = jnp.dot(rows, weights, preferred_element_type=jnp.float32)
        scaled = output_cotangent.astype(jnp.float32) * gain_vec
        squares = lax.optimization_barrier(jnp.sum(keys * keys, axis=1))
        cross = lax.optimization_barrier(jnp.sum(scaled * keys, axis=1))
        inv = 1.0 / jnp.sqrt(squares / KEY_FEATURES + norm_eps)
        normalized_keys = keys * inv[:, None]
        key_grad = (inv[:, None] * (scaled - normalized_keys * (inv * cross / KEY_FEATURES)[:, None])).astype(jnp.bfloat16)
        w_grad = jnp.dot(rows.T, key_grad, preferred_element_type=jnp.float32).astype(jnp.bfloat16)
        gain_gradient = lax.optimization_barrier(jnp.sum(output_cotangent.astype(jnp.float32) * normalized_keys, axis=0)).reshape(KEY_HEADS, HEAD_WIDTH).T
        blocked_k = key_grad.reshape(TOK_DEV, N_TENSOR, width).astype(jnp.float32)
        terms = jnp.einsum('tsw,dsw->std', blocked_k, blocked_w).astype(jnp.bfloat16)
        terms = lax.optimization_barrier(terms)
        in_grad = lax.optimization_barrier(jnp.sum(terms.astype(jnp.float32), axis=0)).astype(jnp.bfloat16)
        return (in_grad, w_grad, gain_gradient)
    in_grads, w_grads, g_grads = lax.map(one_group, (token_features.reshape(N_DP, TOK_DEV, D), key_cotangent.reshape(N_DP, TOK_DEV, KEY_FEATURES)))
    summed_w = lax.optimization_barrier(jnp.sum(weight_grad_prev.astype(jnp.float32), axis=0))
    summed_g = lax.optimization_barrier(jnp.sum(prior_gain_gradient, axis=0))
    new_weight, new_weight_first, new_weight_second = adamw(weight_master, weight_first, weight_second, summed_w, weight_decay)
    new_gain, new_gain_first, new_gain_second = adamw(gain_master_copy, gain_first_moment, gain_second_moment, summed_g, 0.0)
    return (in_grads.reshape(TOKENS, D), w_grads, g_grads, new_weight, new_weight_first, new_weight_second, new_gain, new_gain_first, new_gain_second)
```

```python
import jax
import jax.numpy as jnp
from jax import lax
from jax.sharding import Mesh, PartitionSpec as P

HEAD_WIDTH = 128
KEY_FEATURES = 1024

beta_one = 0.9
beta_two = 0.95
corr_one = 1.0 - 0.9**8
corr_two = 1.0 - 0.95**8
learn_rate = 0.02
weight_decay = 0.1
adam_eps = 1e-08
norm_eps = 1e-06

NZ, NYL, NC, NX, NYH = 8, 4, 2, 4, 2
ROWS = 80
EXT = 88
SWAP = [(0, 1), (1, 0)]
f32, bf16 = jnp.float32, jnp.bfloat16


def adamw(param, first, second, grad, decay):
    first_new = beta_one * first + (1.0 - beta_one) * grad
    second_new = beta_two * second + (1.0 - beta_two) * grad * grad
    update = first_new / corr_one / (jnp.sqrt(second_new / corr_two) + adam_eps)
    return (param - learn_rate * (update + decay * param), first_new, second_new)


def pick(array, index, axis):
    return lax.dynamic_index_in_dim(array, index, axis, keepdims=False)


def ordered(mine, other, index):
    return jnp.where(index == 0, jnp.stack([mine, other]), jnp.stack([other, mine]))


def local(
    token_features,
    key_cotangent,
    weight_master,
    weight_first,
    weight_second,
    gain_master_copy,
    gain_first_moment,
    gain_second_moment,
    weight_grad_prev,
    prior_gain_gradient,
):
    c = lax.axis_index("c")
    yh = lax.axis_index("yh")
    own, width = token_features.shape
    half = NX * own

    prev = weight_grad_prev.reshape(NZ * NYL, NC, ROWS, 128)
    gain_prev = prior_gain_gradient.reshape(NZ * NYL, NC, 2)
    hi = gain_prev.astype(bf16)
    mid = (gain_prev - hi.astype(f32)).astype(bf16)
    low = (gain_prev - hi.astype(f32) - mid.astype(f32)).astype(bf16)
    split = jnp.concatenate([hi, mid, low], axis=-1)[:, :, None, :]
    split = jnp.pad(split, ((0, 0), (0, 0), (0, EXT - ROWS - 1), (0, 128 - 6)))
    keep = jnp.concatenate([pick(prev, c, 1), pick(split, c, 1)], axis=1)
    give = jnp.concatenate([pick(prev, 1 - c, 1), pick(split, 1 - c, 1)], axis=1)
    got = lax.ppermute(give, "c", SWAP)
    pair = keep.astype(f32) + got.astype(f32)
    sum_z = lax.psum_scatter(pair, "z", scatter_dimension=0, tiled=True)
    sum_all = lax.psum_scatter(sum_z, "yl", scatter_dimension=0, tiled=True)[0]

    gain_row = jnp.pad(gain_master_copy.astype(bf16).reshape(1, 2), ((0, EXT - ROWS - 1), (0, 126)))
    shard = jnp.concatenate([weight_master.astype(bf16), gain_row], axis=0)
    group = ("z", "yh", "yl")
    many = NZ * NYH * NYL
    gathered = lax.all_to_all(
        jnp.broadcast_to(shard[None], (many, EXT, 128)), group, 0, 0, tiled=True
    )
    gathered_other = lax.ppermute(gathered, "c", SWAP)
    both = ordered(gathered, gathered_other, c).reshape(NC, NZ, NYH, NYL, EXT, 128)
    both = both.transpose(2, 1, 3, 0, 4, 5)
    weight_two = both[:, :, :, :, :ROWS].reshape(NYH, width, 128)
    gain_two = both[:, :, :, :, ROWS, :2].reshape(NYH, 128).astype(f32)

    cot = key_cotangent.reshape(NX, NYH, own, 128)
    cot_got = lax.ppermute(pick(cot, 1 - yh, 1), "yh", SWAP)
    cot_two = ordered(pick(cot, yh, 1), cot_got, yh).reshape(NYH, half, 128).astype(f32)

    rows = lax.all_gather(token_features, "x", axis=0, tiled=True)
    partner = lax.ppermute(token_features, "yh", SWAP)
    rows_partner = lax.all_gather(partner, "x", axis=0, tiled=True)

    keys = [jnp.dot(rows, weight_two[h], preferred_element_type=f32) for h in range(NYH)]
    scaled = [cot_two[h] * gain_two[h] for h in range(NYH)]
    sums = jnp.stack(
        [
            sum(jnp.sum(k * k, axis=1) for k in keys),
            sum(jnp.sum(s * k, axis=1) for s, k in zip(scaled, keys)),
        ]
    )
    sums = lax.all_to_all(jnp.broadcast_to(sums[None], (NX, 2, half)), "x", 0, 0, tiled=True)
    squares, cross = jnp.sum(sums, axis=0)
    inv = 1.0 / jnp.sqrt(squares / KEY_FEATURES + norm_eps)
    normed = [k * inv[:, None] for k in keys]
    factor = (inv * cross / KEY_FEATURES)[:, None]
    grads = [(inv[:, None] * (s - n * factor)).astype(bf16) for s, n in zip(scaled, normed)]
    gain_terms = jnp.stack([jnp.sum(cot_two[h] * normed[h], axis=0) for h in range(NYH)])

    terms = sum(
        lax.dot_general(grads[h], weight_two[h], (((1,), (1,)), ((), ())), preferred_element_type=f32)
        for h in range(NYH)
    )
    received = lax.all_to_all(terms.astype(bf16).reshape(NX, own, width), "x", 0, 0, tiled=True)
    input_grad = jnp.sum(received.astype(f32), axis=0).astype(bf16)

    both_grads = jnp.stack(grads)
    grad_partner = lax.ppermute(pick(both_grads, 1 - yh, 0), "yh", SWAP)
    gain_partner = lax.ppermute(pick(gain_terms, 1 - yh, 0), "yh", SWAP)
    contract = (((0,), (0,)), ((), ()))
    weight_grad = (
        lax.dot_general(rows, pick(both_grads, yh, 0), contract, preferred_element_type=f32)
        + lax.dot_general(rows_partner, grad_partner, contract, preferred_element_type=f32)
    ).astype(bf16)[None]
    gain_grad = (pick(gain_terms, yh, 0) + gain_partner).reshape(1, 128, 1)

    summed_w = sum_all[:ROWS]
    summed_g = (sum_all[ROWS, 0:2] + sum_all[ROWS, 2:4] + sum_all[ROWS, 4:6]).reshape(2, 1)
    new_weight = adamw(weight_master, weight_first, weight_second, summed_w, weight_decay)
    new_gain = adamw(gain_master_copy, gain_first_moment, gain_second_moment, summed_g, 0.0)
    return (input_grad, weight_grad, gain_grad, *new_weight, *new_gain)


def solution(mesh):
    fine = Mesh(mesh.devices.reshape(NZ, NYL, NC, NX, NYH), ("z", "yl", "c", "x", "yh"))
    dp, tensor = ("z", "yl", "c"), ("x", "yh")
    state = P(dp, tensor)
    stacked = P(dp, None, tensor)
    tokens = P(dp + tensor, None)
    return jax.shard_map(
        local,
        mesh=fine,
        in_specs=(tokens,) + (state,) * 7 + (stacked, stacked),
        out_specs=(tokens, stacked, stacked) + (state,) * 6,
        check_vma=False,
    )
```

```python
import jax
import jax.numpy as jnp
from jax import lax
from jax.sharding import Mesh, PartitionSpec as P

HEAD_WIDTH = 128
KEY_FEATURES = 1024

beta_one = 0.9
beta_two = 0.95
corr_one = 1.0 - 0.9**8
corr_two = 1.0 - 0.95**8
learn_rate = 0.02
weight_decay = 0.1
adam_eps = 1e-08
norm_eps = 1e-06

NZ, NYL, NC, NX, NYH = 8, 4, 2, 4, 2
ROWS = 80
EXT = 88
SWAP = [(0, 1), (1, 0)]
f32, bf16 = jnp.float32, jnp.bfloat16


def adamw(param, first, second, grad, decay):
    first_new = beta_one * first + (1.0 - beta_one) * grad
    second_new = beta_two * second + (1.0 - beta_two) * grad * grad
    update = first_new / corr_one / (jnp.sqrt(second_new / corr_two) + adam_eps)
    return (param - learn_rate * (update + decay * param), first_new, second_new)


def pick(array, index, axis):
    return lax.dynamic_index_in_dim(array, index, axis, keepdims=False)


def ordered(mine, other, index):
    return jnp.where(index == 0, jnp.stack([mine, other]), jnp.stack([other, mine]))


def split3(row, count):
    hi = row.astype(bf16)
    mid = (row - hi.astype(f32)).astype(bf16)
    low = (row - hi.astype(f32) - mid.astype(f32)).astype(bf16)
    index = lax.broadcasted_iota(jnp.int32, (count, 128), 0)
    zero = jnp.zeros((), bf16)
    rest = jnp.where(index == 2, mid, jnp.where(index == 3, low, zero))
    return jnp.where(index == 1, hi, rest)


def gather_x(block):
    return lax.all_gather(jnp.pad(block, ((0, 8), (0, 0))), "x", axis=0)


def used_rows(gathered, own):
    return gathered[:, :own].reshape(-1, gathered.shape[2])


def exchange_x(block_for, mine):
    return [mine] + [
        lax.ppermute(block_for(d), "x", [(i, (i + d) % NX) for i in range(NX)])
        for d in (2, 1, 3)
    ]


def local(
    token_features,
    key_cotangent,
    weight_master,
    weight_first,
    weight_second,
    gain_master_copy,
    gain_first_moment,
    gain_second_moment,
    weight_grad_prev,
    prior_gain_gradient,
):
    c = lax.axis_index("c")
    x = lax.axis_index("x")
    yh = lax.axis_index("yh")
    dp = lax.axis_index(("z", "yl", "c"))
    own, width = token_features.shape
    half = NX * own

    cot = key_cotangent.reshape(NX, NYH, own, 128)
    give_cot = pick(cot, 1 - yh, 1)
    packed = jnp.concatenate([token_features] + [give_cot[i] for i in range(NX)], axis=1)
    packed = lax.ppermute(packed, "yh", SWAP)
    partner = packed[:, :width]
    cot_got = packed[:, width:].reshape(own, NX, 128).transpose(1, 0, 2)

    place = lax.broadcasted_iota(jnp.int32, (EXT - ROWS, 128), 1)
    first = lax.broadcasted_iota(jnp.int32, (EXT - ROWS, 128), 0) == 0
    two = gain_master_copy.astype(bf16)
    zero = jnp.zeros((), bf16)
    gain_row = jnp.where(first & (place == 2 * dp), two[0, 0], zero)
    gain_row = jnp.where(first & (place == 2 * dp + 1), two[1, 0], gain_row)
    gain_row = gain_row + split3(prior_gain_gradient.reshape(1, 128), EXT - ROWS)
    shard = jnp.concatenate([weight_master.astype(bf16), gain_row], axis=0)
    shard, packed = lax.optimization_barrier((shard, packed))
    group = ("z", "yh", "yl")
    many = NZ * NYH * NYL
    gathered = lax.all_to_all(
        jnp.broadcast_to(shard[None], (many, EXT, 128)), group, 0, 0, tiled=True
    )

    rows = used_rows(gather_x(token_features), own)
    rows_partner = gather_x(partner)

    prev = weight_grad_prev.reshape(NZ * NYL * NC, ROWS, 128)
    prev, gathered = lax.optimization_barrier((prev, gathered))
    arrived = lax.all_to_all(prev, ("z", "yl", "c"), 0, 0, tiled=True)

    gathered_other = lax.ppermute(gathered, "c", SWAP)
    both = ordered(gathered, gathered_other, c).reshape(NC, NZ, NYH, NYL, EXT, 128)
    both = both.transpose(2, 1, 3, 0, 4, 5)
    weight_two = both[:, :, :, :, :ROWS].reshape(NYH, width, 128)
    extra = jnp.sum(both[:, :, :, :, ROWS:].astype(f32), axis=(1, 2, 3))
    gain_two = extra[:, 0]
    summed_g = jnp.sum(pick(extra, yh, 0)[1:4], axis=0)

    cot_two = ordered(pick(cot, yh, 1), cot_got, yh).reshape(NYH, half, 128).astype(f32)


    keys = [jnp.dot(rows, weight_two[h], preferred_element_type=f32) for h in range(NYH)]
    scaled = [cot_two[h] * gain_two[h] for h in range(NYH)]
    sums = jnp.stack(
        [
            sum(jnp.sum(k * k, axis=1) for k in keys),
            sum(jnp.sum(s * k, axis=1) for s, k in zip(scaled, keys)),
        ]
    )
    squares, cross = lax.psum(sums, "x")
    inv = 1.0 / jnp.sqrt(squares / KEY_FEATURES + norm_eps)
    normed = [k * inv[:, None] for k in keys]
    factor = (inv * cross / KEY_FEATURES)[:, None]
    grads = [(inv[:, None] * (s - n * factor)).astype(bf16) for s, n in zip(scaled, normed)]
    gain_terms = jnp.stack([jnp.sum(cot_two[h] * normed[h], axis=0) for h in range(NYH)])

    terms = sum(
        lax.dot_general(grads[h], weight_two[h], (((1,), (1,)), ((), ())), preferred_element_type=f32)
        for h in range(NYH)
    )
    terms = terms.astype(bf16).reshape(NX, own, width)
    received = exchange_x(lambda d: pick(terms, lax.rem(x + d, NX), 0), pick(terms, x, 0))
    input_grad = sum(block.astype(f32) for block in received).astype(bf16)

    both_grads = jnp.stack(grads)
    give = jnp.concatenate([both_grads[0], split3(gain_terms[0:1], 8)]), jnp.concatenate(
        [both_grads[1], split3(gain_terms[1:2], 8)]
    )
    got = lax.ppermute(jnp.where(yh == 0, give[1], give[0]), "yh", SWAP)
    rows_partner, got, input_grad = lax.optimization_barrier((rows_partner, got, input_grad))
    rows_partner = used_rows(rows_partner, own)
    contract = (((0,), (0,)), ((), ()))
    weight_grad = (
        lax.dot_general(rows, pick(both_grads, yh, 0), contract, preferred_element_type=f32)
        + lax.dot_general(rows_partner, got[:half], contract, preferred_element_type=f32)
    ).astype(bf16)[None]
    gain_partner = jnp.sum(got[half:].astype(f32), axis=0)
    gain_grad = (pick(gain_terms, yh, 0) + gain_partner).reshape(1, 128, 1)

    arrived, input_grad = lax.optimization_barrier((arrived, input_grad))
    summed_w = jnp.sum(arrived.astype(f32), axis=0)
    summed_g = lax.dynamic_slice(summed_g, (2 * dp,), (2,)).reshape(2, 1)
    new_weight = adamw(weight_master, weight_first, weight_second, summed_w, weight_decay)
    new_gain = adamw(gain_master_copy, gain_first_moment, gain_second_moment, summed_g, 0.0)
    return (input_grad, weight_grad, gain_grad, *new_weight, *new_gain)


def solution(mesh):
    fine = Mesh(mesh.devices.reshape(NZ, NYL, NC, NX, NYH), ("z", "yl", "c", "x", "yh"))
    dp, tensor = ("z", "yl", "c"), ("x", "yh")
    state = P(dp, tensor)
    stacked = P(dp, None, tensor)
    tokens = P(dp + tensor, None)
    return jax.shard_map(
        local,
        mesh=fine,
        in_specs=(tokens,) + (state,) * 7 + (stacked, stacked),
        out_specs=(tokens, stacked, stacked) + (state,) * 6,
        check_vma=False,
    )
```

```python
import jax
import jax.numpy as jnp
from jax import lax
from jax.experimental import pallas as pl
from jax.experimental.pallas import tpu as pltpu
from jax.sharding import Mesh, PartitionSpec as P

HEAD_WIDTH = 128
KEY_FEATURES = 1024

beta_one = 0.9
beta_two = 0.95
corr_one = 1.0 - 0.9**8
corr_two = 1.0 - 0.95**8
learn_rate = 0.02
weight_decay = 0.1
adam_eps = 1e-08
norm_eps = 1e-06

NZ, NYL, NC, NX, NYH = 8, 4, 2, 4, 2
ROWS = 80
EXT = 88
SWAP = [(0, 1), (1, 0)]
f32, bf16 = jnp.float32, jnp.bfloat16


def adamw(param, first, second, grad, decay):
    first_new = beta_one * first + (1.0 - beta_one) * grad
    second_new = beta_two * second + (1.0 - beta_two) * grad * grad
    update = first_new / corr_one / (jnp.sqrt(second_new / corr_two) + adam_eps)
    return (param - learn_rate * (update + decay * param), first_new, second_new)


def pick(array, index, axis):
    return lax.dynamic_index_in_dim(array, index, axis, keepdims=False)


def ordered(mine, other, index):
    return jnp.where(index == 0, jnp.stack([mine, other]), jnp.stack([other, mine]))


def split3(row, count):
    hi = row.astype(bf16)
    mid = (row - hi.astype(f32)).astype(bf16)
    low = (row - hi.astype(f32) - mid.astype(f32)).astype(bf16)
    index = lax.broadcasted_iota(jnp.int32, (count, 128), 0)
    zero = jnp.zeros((), bf16)
    rest = jnp.where(index == 2, mid, jnp.where(index == 3, low, zero))
    return jnp.where(index == 1, hi, rest)


def prepare(place_ref, gain_ref, prior_ref, weight_ref, out_ref):
    lane = lax.broadcasted_iota(jnp.int32, (EXT - ROWS, 128), 1)
    row = lax.broadcasted_iota(jnp.int32, (EXT - ROWS, 128), 0)
    at = 2 * place_ref[0]
    gains = jnp.where(lane == at, gain_ref[0, 0], jnp.where(lane == at + 1, gain_ref[1, 0], 0.0))
    prior = jnp.broadcast_to(prior_ref[...], lane.shape)
    hi = prior.astype(bf16).astype(f32)
    mid = (prior - hi).astype(bf16).astype(f32)
    low = prior - hi - mid
    extra = jnp.where(row == 1, hi, jnp.where(row == 2, mid, jnp.where(row == 3, low, 0.0)))
    extra = jnp.where(row == 0, gains, extra)
    block = jnp.concatenate([weight_ref[...], extra], axis=0).astype(bf16)
    out_ref[...] = jnp.broadcast_to(block[None], out_ref.shape)


def exchange_x(block_for, mine):
    return [mine] + [
        lax.ppermute(block_for(d), "x", [(i, (i + d) % NX) for i in range(NX)])
        for d in (2, 1, 3)
    ]


def local(
    token_features,
    key_cotangent,
    weight_master,
    weight_first,
    weight_second,
    gain_master_copy,
    gain_first_moment,
    gain_second_moment,
    weight_grad_prev,
    prior_gain_gradient,
):
    c = lax.axis_index("c")
    x = lax.axis_index("x")
    yh = lax.axis_index("yh")
    dp = lax.axis_index(("z", "yl", "c"))
    own, width = token_features.shape
    half = NX * own

    partner = lax.ppermute(token_features, "yh", SWAP)

    group = ("z", "yh", "yl")
    many = NZ * NYH * NYL
    shards = pl.pallas_call(
        prepare,
        out_shape=jax.ShapeDtypeStruct((many, EXT, 128), bf16),
        in_specs=[
            pl.BlockSpec(memory_space=pltpu.SMEM),
            pl.BlockSpec(memory_space=pltpu.SMEM),
            pl.BlockSpec(memory_space=pltpu.VMEM),
            pl.BlockSpec(memory_space=pltpu.VMEM),
        ],
        out_specs=pl.BlockSpec(memory_space=pltpu.VMEM),
        compiler_params=pltpu.CompilerParams(vmem_limit_bytes=16 * 1024 * 1024),
    )(dp.reshape(1), gain_master_copy, prior_gain_gradient.reshape(1, 128), weight_master)
    shards, partner = lax.optimization_barrier((shards, partner))
    gathered = lax.all_to_all(shards, group, 0, 0, tiled=True)

    rows = jnp.concatenate([token_features, partner], axis=0)
    rows = lax.all_gather(rows, "x", axis=0, tiled=True)

    cot = key_cotangent.reshape(NX, NYH, own, 128)
    cot_got = lax.ppermute(pick(cot, 1 - yh, 1), "yh", SWAP)
    gathered, cot_got = lax.optimization_barrier((gathered, cot_got))
    cot_two = ordered(pick(cot, yh, 1), cot_got, yh).reshape(NYH, half, 128).astype(f32)

    prev = weight_grad_prev.reshape(NZ * NYL * NC, ROWS, 128)
    prev, gathered = lax.optimization_barrier((prev, gathered))
    arrived = lax.all_to_all(prev, ("z", "yl", "c"), 0, 0, tiled=True)

    gathered_other = lax.ppermute(gathered, "c", SWAP)
    both = ordered(gathered, gathered_other, c).reshape(NC, NZ, NYH, NYL, EXT, 128)
    both = both.transpose(2, 1, 3, 0, 4, 5)
    weight_two = both[:, :, :, :, :ROWS].reshape(NYH, width, 128)
    extra = jnp.sum(both[:, :, :, :, ROWS:].astype(f32), axis=(1, 2, 3))
    gain_two = extra[:, 0]
    summed_g = jnp.sum(pick(extra, yh, 0)[1:4], axis=0)

    keys = [jnp.dot(rows, weight_two[h], preferred_element_type=f32) for h in range(NYH)]
    keys = [k.reshape(NX, NYH, own, 128)[:, 0].reshape(half, 128) for k in keys]
    scaled = [cot_two[h] * gain_two[h] for h in range(NYH)]
    sums = jnp.stack(
        [
            sum(jnp.sum(k * k, axis=1) for k in keys),
            sum(jnp.sum(s * k, axis=1) for s, k in zip(scaled, keys)),
        ]
    )
    squares, cross = lax.psum(sums, "x")
    inv = 1.0 / jnp.sqrt(squares / KEY_FEATURES + norm_eps)
    normed = [k * inv[:, None] for k in keys]
    factor = (inv * cross / KEY_FEATURES)[:, None]
    grads = [(inv[:, None] * (s - n * factor)).astype(bf16) for s, n in zip(scaled, normed)]
    gain_terms = jnp.stack([jnp.sum(cot_two[h] * normed[h], axis=0) for h in range(NYH)])

    terms = sum(
        lax.dot_general(grads[h], weight_two[h], (((1,), (1,)), ((), ())), preferred_element_type=f32)
        for h in range(NYH)
    )
    terms = terms.astype(bf16).reshape(NX, own, width)
    received = exchange_x(lambda d: pick(terms, lax.rem(x + d, NX), 0), pick(terms, x, 0))
    input_grad = sum(block.astype(f32) for block in received).astype(bf16)

    both_grads = jnp.stack(grads)
    give = jnp.concatenate([both_grads[0], split3(gain_terms[0:1], 8)]), jnp.concatenate(
        [both_grads[1], split3(gain_terms[1:2], 8)]
    )
    got = lax.ppermute(jnp.where(yh == 0, give[1], give[0]), "yh", SWAP)
    got, input_grad = lax.optimization_barrier((got, input_grad))
    kept = pick(both_grads, yh, 0).reshape(NX, 1, own, 128)
    group_grad = jnp.concatenate([kept, got[:half].reshape(NX, 1, own, 128)], axis=1)
    weight_grad = lax.dot_general(
        rows, group_grad.reshape(-1, 128), (((0,), (0,)), ((), ())), preferred_element_type=f32
    ).astype(bf16)[None]
    gain_partner = jnp.sum(got[half:].astype(f32), axis=0)
    gain_grad = (pick(gain_terms, yh, 0) + gain_partner).reshape(1, 128, 1)

    arrived, input_grad = lax.optimization_barrier((arrived, input_grad))
    summed_w = jnp.sum(arrived.astype(f32), axis=0)
    summed_g = lax.dynamic_slice(summed_g, (2 * dp,), (2,)).reshape(2, 1)
    new_weight = adamw(weight_master, weight_first, weight_second, summed_w, weight_decay)
    new_gain = adamw(gain_master_copy, gain_first_moment, gain_second_moment, summed_g, 0.0)
    return (input_grad, weight_grad, gain_grad, *new_weight, *new_gain)


def solution(mesh):
    fine = Mesh(mesh.devices.reshape(NZ, NYL, NC, NX, NYH), ("z", "yl", "c", "x", "yh"))
    dp, tensor = ("z", "yl", "c"), ("x", "yh")
    state = P(dp, tensor)
    stacked = P(dp, None, tensor)
    tokens = P(dp + tensor, None)
    return jax.shard_map(
        local,
        mesh=fine,
        in_specs=(tokens,) + (state,) * 7 + (stacked, stacked),
        out_specs=(tokens, stacked, stacked) + (state,) * 6,
        check_vma=False,
    )
```

```python
import jax
import jax.numpy as jnp
from jax import lax
from jax.experimental import pallas as pl
from jax.experimental.pallas import tpu as pltpu
from jax.sharding import Mesh, PartitionSpec as P

HEAD_WIDTH = 128
KEY_FEATURES = 1024

beta_one = 0.9
beta_two = 0.95
corr_one = 1.0 - 0.9**8
corr_two = 1.0 - 0.95**8
learn_rate = 0.02
weight_decay = 0.1
adam_eps = 1e-08
norm_eps = 1e-06

NZ, NYL, NC, NX, NYH = 8, 4, 2, 4, 2
ROWS = 80
EXT = 88
AXES = ("z", "yl", "c", "x", "yh")
SWAP = [(0, 1), (1, 0)]
f32, bf16 = jnp.float32, jnp.bfloat16


def adamw(param, first, second, grad, decay):
    first_new = beta_one * first + (1.0 - beta_one) * grad
    second_new = beta_two * second + (1.0 - beta_two) * grad * grad
    update = first_new / corr_one / (jnp.sqrt(second_new / corr_two) + adam_eps)
    return (param - learn_rate * (update + decay * param), first_new, second_new)


def pick(array, index, axis):
    return lax.dynamic_index_in_dim(array, index, axis, keepdims=False)


def ordered(mine, other, index):
    return jnp.where(index == 0, jnp.stack([mine, other]), jnp.stack([other, mine]))


def split3(row, count):
    hi = row.astype(bf16)
    mid = (row - hi.astype(f32)).astype(bf16)
    low = (row - hi.astype(f32) - mid.astype(f32)).astype(bf16)
    index = lax.broadcasted_iota(jnp.int32, (count, 128), 0)
    zero = jnp.zeros((), bf16)
    rest = jnp.where(index == 2, mid, jnp.where(index == 3, low, zero))
    return jnp.where(index == 1, hi, rest)


def rings(core, z_varies):
    def at(z, y, x):
        return (((z * NYL + y % NYL) * NC + core) * NX + x) * NYH + y // NYL

    spread, fixed = (NZ, NYH * NYL) if z_varies else (NYH * NYL, NZ)
    return [
        [at(i, j, x) if z_varies else at(j, i, x) for i in range(spread)]
        for x in range(NX)
        for j in range(fixed)
    ]


def prepare(place_ref, gain_ref, prior_ref, weight_ref, out_ref):
    lane = lax.broadcasted_iota(jnp.int32, (EXT - ROWS, 128), 1)
    row = lax.broadcasted_iota(jnp.int32, (EXT - ROWS, 128), 0)
    at = 2 * place_ref[0]
    gains = jnp.where(lane == at, gain_ref[0, 0], jnp.where(lane == at + 1, gain_ref[1, 0], 0.0))
    prior = jnp.broadcast_to(prior_ref[...], lane.shape)
    hi = prior.astype(bf16).astype(f32)
    mid = (prior - hi).astype(bf16).astype(f32)
    low = prior - hi - mid
    extra = jnp.where(row == 1, hi, jnp.where(row == 2, mid, jnp.where(row == 3, low, 0.0)))
    extra = jnp.where(row == 0, gains, extra)
    block = jnp.concatenate([weight_ref[...], extra], axis=0).astype(bf16)
    out_ref[...] = jnp.broadcast_to(block[None], out_ref.shape)


def exchange_x(block_for, mine):
    return [mine] + [
        lax.ppermute(block_for(d), "x", [(i, (i + d) % NX) for i in range(NX)])
        for d in (2, 1, 3)
    ]


def local(
    token_features,
    key_cotangent,
    weight_master,
    weight_first,
    weight_second,
    gain_master_copy,
    gain_first_moment,
    gain_second_moment,
    weight_grad_prev,
    prior_gain_gradient,
):
    c = lax.axis_index("c")
    x = lax.axis_index("x")
    yh = lax.axis_index("yh")
    dp = lax.axis_index(("z", "yl", "c"))
    own, width = token_features.shape
    half = NX * own

    partner = lax.ppermute(token_features, "yh", SWAP)

    ring = NYH * NYL
    shards = pl.pallas_call(
        prepare,
        out_shape=jax.ShapeDtypeStruct((NZ, EXT, 128), bf16),
        in_specs=[
            pl.BlockSpec(memory_space=pltpu.SMEM),
            pl.BlockSpec(memory_space=pltpu.SMEM),
            pl.BlockSpec(memory_space=pltpu.VMEM),
            pl.BlockSpec(memory_space=pltpu.VMEM),
        ],
        out_specs=pl.BlockSpec(memory_space=pltpu.VMEM),
        compiler_params=pltpu.CompilerParams(vmem_limit_bytes=16 * 1024 * 1024),
    )(dp.reshape(1), gain_master_copy, prior_gain_gradient.reshape(1, 128), weight_master)
    along_z, along_y = [rings(core, True) for core in range(NC)], [rings(core, False) for core in range(NC)]
    first = lax.all_to_all(
        shards, AXES, 0, 0, tiled=True, axis_index_groups=along_z[0] + along_y[1]
    )
    first, partner = lax.optimization_barrier((first, partner))
    gathered = lax.all_to_all(
        jnp.broadcast_to(first.reshape(1, -1, 128), (ring, NZ * EXT, 128)),
        AXES, 0, 0, tiled=True, axis_index_groups=along_y[0] + along_z[1],
    )

    rows = jnp.concatenate([token_features, partner], axis=0)
    rows = lax.all_gather(rows, "x", axis=0, tiled=True)

    cot = key_cotangent.reshape(NX, NYH, own, 128)
    cot_got = lax.ppermute(pick(cot, 1 - yh, 1), "yh", SWAP)
    gathered, cot_got = lax.optimization_barrier((gathered, cot_got))
    cot_two = ordered(pick(cot, yh, 1), cot_got, yh).reshape(NYH, half, 128).astype(f32)

    prev = weight_grad_prev.reshape(NZ * NYL, NC, ROWS, 128)
    other_core = lax.ppermute(pick(prev, 1 - c, 1), "c", SWAP)
    pair = (pick(prev, c, 1).astype(f32) + other_core.astype(f32)).astype(bf16)
    pair, gathered = lax.optimization_barrier((pair, gathered))
    arrived = lax.all_to_all(pair, ("z", "yl"), 0, 0, tiled=True)

    gathered_other = lax.ppermute(gathered, "c", SWAP)
    both = ordered(gathered, gathered_other, c)
    core_0 = both[0].reshape(NYH, NYL, NZ, EXT, 128).transpose(0, 2, 1, 3, 4)
    core_1 = both[1].reshape(NZ, NYH, NYL, EXT, 128).transpose(1, 0, 2, 3, 4)
    both = jnp.stack([core_0, core_1], axis=3)
    weight_two = both[:, :, :, :, :ROWS].reshape(NYH, width, 128)
    extra = jnp.sum(both[:, :, :, :, ROWS:].astype(f32), axis=(1, 2, 3))
    gain_two = extra[:, 0]
    summed_g = jnp.sum(pick(extra, yh, 0)[1:4], axis=0)

    keys = [jnp.dot(rows, weight_two[h], preferred_element_type=f32) for h in range(NYH)]
    keys = [k.reshape(NX, NYH, own, 128)[:, 0].reshape(half, 128) for k in keys]
    scaled = [cot_two[h] * gain_two[h] for h in range(NYH)]
    sums = jnp.stack(
        [
            sum(jnp.sum(k * k, axis=1) for k in keys),
            sum(jnp.sum(s * k, axis=1) for s, k in zip(scaled, keys)),
        ]
    )
    squares, cross = lax.psum(sums, "x")
    inv = 1.0 / jnp.sqrt(squares / KEY_FEATURES + norm_eps)
    normed = [k * inv[:, None] for k in keys]
    factor = (inv * cross / KEY_FEATURES)[:, None]
    grads = [(inv[:, None] * (s - n * factor)).astype(bf16) for s, n in zip(scaled, normed)]
    gain_terms = jnp.stack([jnp.sum(cot_two[h] * normed[h], axis=0) for h in range(NYH)])

    terms = sum(
        lax.dot_general(grads[h], weight_two[h], (((1,), (1,)), ((), ())), preferred_element_type=f32)
        for h in range(NYH)
    )
    terms = terms.astype(bf16).reshape(NX, own, width)
    received = exchange_x(lambda d: pick(terms, lax.rem(x + d, NX), 0), pick(terms, x, 0))
    input_grad = sum(block.astype(f32) for block in received).astype(bf16)

    both_grads = jnp.stack(grads)
    give = jnp.concatenate([both_grads[0], split3(gain_terms[0:1], 8)]), jnp.concatenate(
        [both_grads[1], split3(gain_terms[1:2], 8)]
    )
    got = lax.ppermute(jnp.where(yh == 0, give[1], give[0]), "yh", SWAP)
    got, input_grad = lax.optimization_barrier((got, input_grad))
    kept = pick(both_grads, yh, 0).reshape(NX, 1, own, 128)
    group_grad = jnp.concatenate([kept, got[:half].reshape(NX, 1, own, 128)], axis=1)
    weight_grad = lax.dot_general(
        rows, group_grad.reshape(-1, 128), (((0,), (0,)), ((), ())), preferred_element_type=f32
    ).astype(bf16)[None]
    gain_partner = jnp.sum(got[half:].astype(f32), axis=0)
    gain_grad = (pick(gain_terms, yh, 0) + gain_partner).reshape(1, 128, 1)

    arrived, input_grad = lax.optimization_barrier((arrived, input_grad))
    summed_w = jnp.sum(arrived.astype(f32), axis=0)
    summed_g = lax.dynamic_slice(summed_g, (2 * dp,), (2,)).reshape(2, 1)
    new_weight = adamw(weight_master, weight_first, weight_second, summed_w, weight_decay)
    new_gain = adamw(gain_master_copy, gain_first_moment, gain_second_moment, summed_g, 0.0)
    return (input_grad, weight_grad, gain_grad, *new_weight, *new_gain)


def solution(mesh):
    fine = Mesh(mesh.devices.reshape(NZ, NYL, NC, NX, NYH), AXES)
    dp, tensor = ("z", "yl", "c"), ("x", "yh")
    state = P(dp, tensor)
    stacked = P(dp, None, tensor)
    tokens = P(dp + tensor, None)
    return jax.shard_map(
        local,
        mesh=fine,
        in_specs=(tokens,) + (state,) * 7 + (stacked, stacked),
        out_specs=(tokens, stacked, stacked) + (state,) * 6,
        check_vma=False,
    )
```

```python
import jax
import jax.numpy as jnp
from jax import lax
from jax.experimental import pallas as pl
from jax.experimental.pallas import tpu as pltpu
from jax.sharding import Mesh, PartitionSpec as P

HEAD_WIDTH = 128
KEY_FEATURES = 1024

beta_one = 0.9
beta_two = 0.95
corr_one = 1.0 - 0.9**8
corr_two = 1.0 - 0.95**8
learn_rate = 0.02
weight_decay = 0.1
adam_eps = 1e-08
norm_eps = 1e-06

NZ, NYL, NC, NX, NYH = 8, 4, 2, 4, 2
ROWS = 80
EXT = 88
AXES = ("z", "yl", "c", "x", "yh")
SWAP = [(0, 1), (1, 0)]
f32, bf16 = jnp.float32, jnp.bfloat16


def adamw(param, first, second, grad, decay):
    first_new = beta_one * first + (1.0 - beta_one) * grad
    second_new = beta_two * second + (1.0 - beta_two) * grad * grad
    update = first_new / corr_one / (jnp.sqrt(second_new / corr_two) + adam_eps)
    return (param - learn_rate * (update + decay * param), first_new, second_new)


def pick(array, index, axis):
    return lax.dynamic_index_in_dim(array, index, axis, keepdims=False)


def ordered(mine, other, index):
    return jnp.where(index == 0, jnp.stack([mine, other]), jnp.stack([other, mine]))


def split3(row, count):
    hi = row.astype(bf16)
    mid = (row - hi.astype(f32)).astype(bf16)
    low = (row - hi.astype(f32) - mid.astype(f32)).astype(bf16)
    index = lax.broadcasted_iota(jnp.int32, (count, 128), 0)
    zero = jnp.zeros((), bf16)
    rest = jnp.where(index == 2, mid, jnp.where(index == 3, low, zero))
    return jnp.where(index == 1, hi, rest)


def rings(core, z_varies):
    def at(z, y, x):
        return (((z * NYL + y % NYL) * NC + core) * NX + x) * NYH + y // NYL

    spread, fixed = (NZ, NYH * NYL) if z_varies else (NYH * NYL, NZ)
    return [
        [at(i, j, x) if z_varies else at(j, i, x) for i in range(spread)]
        for x in range(NX)
        for j in range(fixed)
    ]


def prepare(place_ref, gain_ref, prior_ref, weight_ref, out_ref):
    lane = lax.broadcasted_iota(jnp.int32, (EXT - ROWS, 128), 1)
    row = lax.broadcasted_iota(jnp.int32, (EXT - ROWS, 128), 0)
    at = 2 * place_ref[0]
    gain = gain_ref[...]
    one, two = (jnp.broadcast_to(gain[:, i : i + 1], lane.shape) for i in range(2))
    gains = jnp.where(lane == at, one, jnp.where(lane == at + 1, two, 0.0))
    prior = jnp.broadcast_to(prior_ref[...], lane.shape)
    hi = prior.astype(bf16).astype(f32)
    mid = (prior - hi).astype(bf16).astype(f32)
    low = prior - hi - mid
    extra = jnp.where(row == 1, hi, jnp.where(row == 2, mid, jnp.where(row == 3, low, 0.0)))
    extra = jnp.where(row == 0, gains, extra)
    block = jnp.concatenate([weight_ref[...], extra], axis=0).astype(bf16)
    out_ref[...] = jnp.broadcast_to(block[None], out_ref.shape)


def exchange(axis, size, block_for, mine):
    return [mine] + [
        lax.ppermute(block_for(d), axis, [(i, (i + d) % size) for i in range(size)])
        for d in (2, 1, 3)
    ]


def local(
    token_features,
    key_cotangent,
    weight_master,
    weight_first,
    weight_second,
    gain_master_copy,
    gain_first_moment,
    gain_second_moment,
    weight_grad_prev,
    prior_gain_gradient,
):
    c = lax.axis_index("c")
    x = lax.axis_index("x")
    yh = lax.axis_index("yh")
    dp = lax.axis_index(("z", "yl", "c"))
    own, width = token_features.shape
    half = NX * own

    partner = lax.ppermute(token_features, "yh", SWAP)

    ring = NYH * NYL
    shards = pl.pallas_call(
        prepare,
        out_shape=jax.ShapeDtypeStruct((NZ, EXT, 128), bf16),
        in_specs=[
            pl.BlockSpec(memory_space=pltpu.SMEM),
            pl.BlockSpec(memory_space=pltpu.VMEM),
            pl.BlockSpec(memory_space=pltpu.VMEM),
            pl.BlockSpec(memory_space=pltpu.VMEM),
        ],
        out_specs=pl.BlockSpec(memory_space=pltpu.VMEM),
        compiler_params=pltpu.CompilerParams(vmem_limit_bytes=16 * 1024 * 1024),
    )(dp.reshape(1), gain_master_copy.T, prior_gain_gradient.reshape(1, 128), weight_master)
    along_z, along_y = [rings(core, True) for core in range(NC)], [rings(core, False) for core in range(NC)]
    first = lax.all_to_all(
        shards, AXES, 0, 0, tiled=True, axis_index_groups=along_z[0] + along_y[1]
    )
    rows = jnp.concatenate([token_features, partner], axis=0)

    prev = weight_grad_prev.reshape(NZ * NYL, NC, ROWS, 128)
    other_core = lax.ppermute(pick(prev, 1 - c, 1), "c", SWAP)
    pair = (pick(prev, c, 1).astype(f32) + other_core.astype(f32)).astype(bf16)

    cot = key_cotangent.reshape(NX, NYH, own, 128)
    cot_got = lax.ppermute(pick(cot, 1 - yh, 1), "yh", SWAP)
    cot_two = ordered(pick(cot, yh, 1), cot_got, yh).reshape(NYH, half, 128).astype(f32)

    first, rows, pair, cot_two = lax.optimization_barrier((first, rows, pair, cot_two))
    rows = lax.all_gather(rows, "x", axis=0, tiled=True)
    gathered = lax.all_to_all(
        jnp.broadcast_to(first.reshape(1, -1, 128), (ring, NZ * EXT, 128)),
        AXES, 0, 0, tiled=True, axis_index_groups=along_y[0] + along_z[1],
    )

    pair, gathered = lax.optimization_barrier((pair, gathered))
    arrived = lax.all_to_all(pair, ("z", "yl"), 0, 0, tiled=True)

    gathered_other = lax.ppermute(gathered, "c", SWAP)
    both = ordered(gathered, gathered_other, c)
    core_0 = both[0].reshape(NYH, NYL, NZ, EXT, 128).transpose(0, 2, 1, 3, 4)
    core_1 = both[1].reshape(NZ, NYH, NYL, EXT, 128).transpose(1, 0, 2, 3, 4)
    both = jnp.stack([core_0, core_1], axis=3)
    weight_two = both[:, :, :, :, :ROWS].reshape(NYH, width, 128)
    extra = jnp.sum(both[:, :, :, :, ROWS:].astype(f32), axis=(1, 2, 3))
    gain_two = extra[:, 0]
    summed_g = jnp.sum(pick(extra, yh, 0)[1:4], axis=0)

    keys = [jnp.dot(rows, weight_two[h], preferred_element_type=f32) for h in range(NYH)]
    keys = [k.reshape(NX, NYH, own, 128)[:, 0].reshape(half, 128) for k in keys]
    scaled = [cot_two[h] * gain_two[h] for h in range(NYH)]
    sums = jnp.stack(
        [
            sum(jnp.sum(k * k, axis=1) for k in keys),
            sum(jnp.sum(s * k, axis=1) for s, k in zip(scaled, keys)),
        ]
    )
    squares, cross = lax.psum(sums, "x")
    inv = 1.0 / jnp.sqrt(squares / KEY_FEATURES + norm_eps)
    normed = [k * inv[:, None] for k in keys]
    factor = (inv * cross / KEY_FEATURES)[:, None]
    grads = [(inv[:, None] * (s - n * factor)).astype(bf16) for s, n in zip(scaled, normed)]
    gain_terms = jnp.stack([jnp.sum(cot_two[h] * normed[h], axis=0) for h in range(NYH)])

    terms = sum(
        lax.dot_general(grads[h], weight_two[h], (((1,), (1,)), ((), ())), preferred_element_type=f32)
        for h in range(NYH)
    )
    terms = terms.astype(bf16).reshape(NX, own, width)
    received = exchange("x", NX, lambda d: pick(terms, lax.rem(x + d, NX), 0), pick(terms, x, 0))
    input_grad = sum(block.astype(f32) for block in received).astype(bf16)

    both_grads = jnp.stack(grads)
    give = jnp.concatenate([both_grads[0], split3(gain_terms[0:1], 8)]), jnp.concatenate(
        [both_grads[1], split3(gain_terms[1:2], 8)]
    )
    got = lax.ppermute(jnp.where(yh == 0, give[1], give[0]), "yh", SWAP)
    got, input_grad = lax.optimization_barrier((got, input_grad))
    kept = pick(both_grads, yh, 0).reshape(NX, 1, own, 128)
    group_grad = jnp.concatenate([kept, got[:half].reshape(NX, 1, own, 128)], axis=1)
    weight_grad = lax.dot_general(
        rows, group_grad.reshape(-1, 128), (((0,), (0,)), ((), ())), preferred_element_type=f32
    ).astype(bf16)[None]
    gain_partner = jnp.sum(got[half:].astype(f32), axis=0)
    gain_grad = (pick(gain_terms, yh, 0) + gain_partner).reshape(1, 128, 1)

    arrived, input_grad = lax.optimization_barrier((arrived, input_grad))
    summed_w = jnp.sum(arrived.astype(f32), axis=0)
    summed_g = lax.dynamic_slice(summed_g, (2 * dp,), (2,)).reshape(2, 1)
    new_weight = adamw(weight_master, weight_first, weight_second, summed_w, weight_decay)
    new_gain = adamw(gain_master_copy, gain_first_moment, gain_second_moment, summed_g, 0.0)
    return (input_grad, weight_grad, gain_grad, *new_weight, *new_gain)


def solution(mesh):
    fine = Mesh(mesh.devices.reshape(NZ, NYL, NC, NX, NYH), AXES)
    dp, tensor = ("z", "yl", "c"), ("x", "yh")
    state = P(dp, tensor)
    stacked = P(dp, None, tensor)
    tokens = P(dp + tensor, None)
    return jax.shard_map(
        local,
        mesh=fine,
        in_specs=(tokens,) + (state,) * 7 + (stacked, stacked),
        out_specs=(tokens, stacked, stacked) + (state,) * 6,
        check_vma=False,
    )
```

```python
import jax
import jax.numpy as jnp
from jax import lax
from jax.experimental import pallas as pl
from jax.experimental.pallas import tpu as pltpu
from jax.sharding import Mesh, PartitionSpec as P

HEAD_WIDTH = 128
KEY_FEATURES = 1024

beta_one = 0.9
beta_two = 0.95
corr_one = 1.0 - 0.9**8
corr_two = 1.0 - 0.95**8
learn_rate = 0.02
weight_decay = 0.1
adam_eps = 1e-08
norm_eps = 1e-06

NZ, NYL, NC, NX, NYH = 8, 4, 2, 4, 2
ROWS = 80
EXT = 88
AXES = ("z", "yl", "c", "x", "yh")
SWAP = [(0, 1), (1, 0)]
f32, bf16 = jnp.float32, jnp.bfloat16


def adamw(param, first, second, grad, decay):
    first_new = beta_one * first + (1.0 - beta_one) * grad
    second_new = beta_two * second + (1.0 - beta_two) * grad * grad
    update = first_new / corr_one / (jnp.sqrt(second_new / corr_two) + adam_eps)
    return (param - learn_rate * (update + decay * param), first_new, second_new)


def pick(array, index, axis):
    return lax.dynamic_index_in_dim(array, index, axis, keepdims=False)


def ordered(mine, other, index):
    return jnp.where(index == 0, jnp.stack([mine, other]), jnp.stack([other, mine]))


def split3(row, count):
    hi = row.astype(bf16)
    mid = (row - hi.astype(f32)).astype(bf16)
    low = (row - hi.astype(f32) - mid.astype(f32)).astype(bf16)
    index = lax.broadcasted_iota(jnp.int32, (count, 128), 0)
    zero = jnp.zeros((), bf16)
    rest = jnp.where(index == 2, mid, jnp.where(index == 3, low, zero))
    return jnp.where(index == 1, hi, rest)


def rings(core, z_varies):
    def at(z, y, x):
        return (((z * NYL + y % NYL) * NC + core) * NX + x) * NYH + y // NYL

    spread, fixed = (NZ, NYH * NYL) if z_varies else (NYH * NYL, NZ)
    return [
        [at(i, j, x) if z_varies else at(j, i, x) for i in range(spread)]
        for x in range(NX)
        for j in range(fixed)
    ]


def prepare(place_ref, gain_ref, prior_ref, weight_ref, out_ref):
    lane = lax.broadcasted_iota(jnp.int32, (EXT - ROWS, 128), 1)
    row = lax.broadcasted_iota(jnp.int32, (EXT - ROWS, 128), 0)
    at = 2 * place_ref[0]
    gain = gain_ref[...]
    one, two = (jnp.broadcast_to(gain[:, i : i + 1], lane.shape) for i in range(2))
    gains = jnp.where(lane == at, one, jnp.where(lane == at + 1, two, 0.0))
    prior = jnp.broadcast_to(prior_ref[...], lane.shape)
    hi = prior.astype(bf16).astype(f32)
    mid = (prior - hi).astype(bf16).astype(f32)
    low = prior - hi - mid
    extra = jnp.where(row == 1, hi, jnp.where(row == 2, mid, jnp.where(row == 3, low, 0.0)))
    extra = jnp.where(row == 0, gains, extra)
    block = jnp.concatenate([weight_ref[...], extra], axis=0).astype(bf16)
    out_ref[...] = jnp.broadcast_to(block[None], out_ref.shape)


def exchange(axis, size, block_for, mine):
    return [mine] + [
        lax.ppermute(block_for(d), axis, [(i, (i + d) % size) for i in range(size)])
        for d in (1, 3, 2)
    ]


def local(
    token_features,
    key_cotangent,
    weight_master,
    weight_first,
    weight_second,
    gain_master_copy,
    gain_first_moment,
    gain_second_moment,
    weight_grad_prev,
    prior_gain_gradient,
):
    c = lax.axis_index("c")
    x = lax.axis_index("x")
    yh = lax.axis_index("yh")
    dp = lax.axis_index(("z", "yl", "c"))
    own, width = token_features.shape
    half = NX * own

    partner = lax.ppermute(token_features, "yh", SWAP)

    ring = NYH * NYL
    shards = pl.pallas_call(
        prepare,
        out_shape=jax.ShapeDtypeStruct((NZ, EXT, 128), bf16),
        in_specs=[
            pl.BlockSpec(memory_space=pltpu.SMEM),
            pl.BlockSpec(memory_space=pltpu.VMEM),
            pl.BlockSpec(memory_space=pltpu.VMEM),
            pl.BlockSpec(memory_space=pltpu.VMEM),
        ],
        out_specs=pl.BlockSpec(memory_space=pltpu.VMEM),
        compiler_params=pltpu.CompilerParams(vmem_limit_bytes=16 * 1024 * 1024),
    )(dp.reshape(1), gain_master_copy.T, prior_gain_gradient.reshape(1, 128), weight_master)
    along_z, along_y = [rings(core, True) for core in range(NC)], [rings(core, False) for core in range(NC)]
    first = lax.all_to_all(
        shards, AXES, 0, 0, tiled=True, axis_index_groups=along_z[0] + along_y[1]
    )
    rows = jnp.concatenate([token_features, partner], axis=0)

    prev = weight_grad_prev.reshape(NZ * NYL, NC, ROWS, 128)
    other_core = lax.ppermute(pick(prev, 1 - c, 1), "c", SWAP)
    pair = (pick(prev, c, 1).astype(f32) + other_core.astype(f32)).astype(bf16)

    cot = key_cotangent.reshape(NX, NYH, own, 128)
    cot_got = lax.ppermute(pick(cot, 1 - yh, 1), "yh", SWAP)
    cot_two = ordered(pick(cot, yh, 1), cot_got, yh).reshape(NYH, half, 128).astype(f32)

    first, rows, pair, cot_two = lax.optimization_barrier((first, rows, pair, cot_two))
    rows = lax.all_gather(rows, "x", axis=0, tiled=True)
    gathered = lax.all_to_all(
        jnp.broadcast_to(first.reshape(1, -1, 128), (ring, NZ * EXT, 128)),
        AXES, 0, 0, tiled=True, axis_index_groups=along_y[0] + along_z[1],
    )

    pair, gathered = lax.optimization_barrier((pair, gathered))
    arrived = lax.all_to_all(pair, ("z", "yl"), 0, 0, tiled=True)

    gathered_other = lax.ppermute(gathered, "c", SWAP)
    both = ordered(gathered, gathered_other, c)
    core_0 = both[0].reshape(NYH, NYL, NZ, EXT, 128).transpose(0, 2, 1, 3, 4)
    core_1 = both[1].reshape(NZ, NYH, NYL, EXT, 128).transpose(1, 0, 2, 3, 4)
    both = jnp.stack([core_0, core_1], axis=3)
    weight_two = both[:, :, :, :, :ROWS].reshape(NYH, width, 128)
    extra = jnp.sum(both[:, :, :, :, ROWS:].astype(f32), axis=(1, 2, 3))
    gain_two = extra[:, 0]
    summed_g = jnp.sum(pick(extra, yh, 0)[1:4], axis=0)

    keys = [jnp.dot(rows, weight_two[h], preferred_element_type=f32) for h in range(NYH)]
    keys = [k.reshape(NX, NYH, own, 128)[:, 0].reshape(half, 128) for k in keys]
    scaled = [cot_two[h] * gain_two[h] for h in range(NYH)]
    sums = jnp.stack(
        [
            sum(jnp.sum(k * k, axis=1) for k in keys),
            sum(jnp.sum(s * k, axis=1) for s, k in zip(scaled, keys)),
        ]
    )
    squares, cross = lax.psum(sums, "x")
    inv = 1.0 / jnp.sqrt(squares / KEY_FEATURES + norm_eps)
    normed = [k * inv[:, None] for k in keys]
    factor = (inv * cross / KEY_FEATURES)[:, None]
    grads = [(inv[:, None] * (s - n * factor)).astype(bf16) for s, n in zip(scaled, normed)]
    gain_terms = jnp.stack([jnp.sum(cot_two[h] * normed[h], axis=0) for h in range(NYH)])

    terms = sum(
        lax.dot_general(grads[h], weight_two[h], (((1,), (1,)), ((), ())), preferred_element_type=f32)
        for h in range(NYH)
    )
    terms = terms.astype(bf16).reshape(NX, own, width)
    received = exchange("x", NX, lambda d: pick(terms, lax.rem(x + d, NX), 0), pick(terms, x, 0))
    input_grad = sum(block.astype(f32) for block in received).astype(bf16)

    both_grads = jnp.stack(grads)
    give = jnp.concatenate([both_grads[0], split3(gain_terms[0:1], 8)]), jnp.concatenate(
        [both_grads[1], split3(gain_terms[1:2], 8)]
    )
    got = lax.ppermute(jnp.where(yh == 0, give[1], give[0]), "yh", SWAP)
    arrived, input_grad = lax.optimization_barrier((arrived, input_grad))
    summed_w = jnp.sum(arrived.astype(f32), axis=0)
    new_weight = adamw(weight_master, weight_first, weight_second, summed_w, weight_decay)
    got, input_grad, new_weight = lax.optimization_barrier((got, input_grad, new_weight))
    kept = pick(both_grads, yh, 0).reshape(NX, 1, own, 128)
    group_grad = jnp.concatenate([kept, got[:half].reshape(NX, 1, own, 128)], axis=1)
    weight_grad = lax.dot_general(
        rows, group_grad.reshape(-1, 128), (((0,), (0,)), ((), ())), preferred_element_type=f32
    ).astype(bf16)[None]
    gain_partner = jnp.sum(got[half:].astype(f32), axis=0)
    gain_grad = (pick(gain_terms, yh, 0) + gain_partner).reshape(1, 128, 1)

    summed_g = lax.dynamic_slice(summed_g, (2 * dp,), (2,)).reshape(2, 1)
    new_gain = adamw(gain_master_copy, gain_first_moment, gain_second_moment, summed_g, 0.0)
    return (input_grad, weight_grad, gain_grad, *new_weight, *new_gain)


def solution(mesh):
    fine = Mesh(mesh.devices.reshape(NZ, NYL, NC, NX, NYH), AXES)
    dp, tensor = ("z", "yl", "c"), ("x", "yh")
    state = P(dp, tensor)
    stacked = P(dp, None, tensor)
    tokens = P(dp + tensor, None)
    return jax.shard_map(
        local,
        mesh=fine,
        in_specs=(tokens,) + (state,) * 7 + (stacked, stacked),
        out_specs=(tokens, stacked, stacked) + (state,) * 6,
        check_vma=False,
    )
```
